32 devices in a mesh: dp: 8 (over y, x, core), mp: 4 (over z).
Axes of the slice: x: 2, y: 2, z: 4, core: 2. Of those that a mesh axis runs over, the one named last changes fastest.
Arguments:
- inputs: float32 [8192, 1024], P(('dp', 'mp')), may hold values from -6 to 6
- doc_ids: int32 [8, 1024], P('dp'), may hold values from 0 to 7, never falling along the last dimension, each value on 1 to 768 neighbouring positions
- cotangent: float32 [8192, 1024], P(('dp', 'mp')), may hold values from -6 to 6
- norm1_gain: float32 [1024], replicated, may hold values from 0.25 to 1.75
- norm2_gain: float32 [1024], replicated, may hold values from 0.25 to 1.75
- qnorm_gain: float32 [64], replicated, may hold values from 0.25 to 1.75
- knorm_gain: float32 [64], replicated, may hold values from 0.25 to 1.75
- q_weight: bfloat16 [1024, 1024], P(None, 'mp'), may hold values from -0.1875 to 0.1875
- k_weight: bfloat16 [1024, 512], P(None, 'mp'), may hold values from -0.1875 to 0.1875
- v_weight: bfloat16 [1024, 512], P(None, 'mp'), may hold values from -0.1875 to 0.1875
- o_weight: bfloat16 [1024, 1024], P('mp'), may hold values from -0.75 to 0.75
- gate_weight: bfloat16 [1024, 4608], P(None, 'mp'), may hold values from -0.1875 to 0.1875
- up_weight: bfloat16 [1024, 4608], P(None, 'mp'), may hold values from -0.1875 to 0.1875
- down_weight: bfloat16 [4608, 1024], P('mp'), may hold values from -0.09375 to 0.09375
Outputs:
- result: float32 [8192, 1024], P(('dp', 'mp'))
- inputs_grad: float32 [8192, 1024], P(('dp', 'mp'))
- norm1_grad: float32 [1024], replicated
- norm2_grad: float32 [1024], replicated
- qnorm_grad: float32 [64], replicated
- knorm_grad: float32 [64], replicated
- q_grad: float32 [1024, 1024], P(None, 'mp')
- k_grad: float32 [1024, 512], P(None, 'mp')
- v_grad: float32 [1024, 512], P(None, 'mp')
- o_grad: float32 [1024, 1024], P('mp')
- gate_grad: float32 [1024, 4608], P(None, 'mp')
- up_grad: float32 [1024, 4608], P(None, 'mp')
- down_grad: float32 [4608, 1024], P('mp')
The draws below stay inside these ranges and needn't reach their ends.
Inputs may be any that keep to these rules, and one draw needn't show every extreme that they name: `doc_ids`: numbers start at 0 in each sequence and never fall along it; each document has 1 to 768 tokens, some exactly 768.
All inputs are finite; a program needn't handle non-finite values.
Results may differ from the reference program's by a relative error of at most 0.018.
Values may be sent and summed in bfloat16 or wider, within the bound.
A program may use at most 128 MiB of HBM per device.

```python
import math
import jax
import jax.numpy as jnp
import numpy as np
from jax import lax

D = 1024
H = 16
KV = 8
HEAD = 64
FF = 4608
TOK_DEV = 1024
SEQS = 8
TOKENS = 8192
DOCS = 8
MOST = 768


def level_of(rng, shape, split, smallest, top_value):
    gain = 1.0
    for position, blocks in split:
        steps = jax.random.uniform(jax.random.fold_in(jax.random.fold_in(rng, 6), position), (blocks,), jnp.float32, smallest / len(split), top_value / len(split))
        gain = gain * jnp.repeat(jnp.exp(steps), shape[position] // blocks).reshape((-1,) + (1,) * (len(shape) - 1 - position))
    return gain


def length_profile(number_of, total, most, skew):
    weights = [(1 << 20) // math.isqrt(rank ** skew) + 1 for rank in range(2, number_of + 1)]
    spare, counts = total - most - (number_of - 1), [1] * (number_of - 1)
    while spare > 0:
        movable = [i for i in range(number_of - 1) if counts[i] < most]
        pool, left = sum([weights[i] for i in movable]), spare
        for i in movable:
            more = min(most - counts[i], max(1, left * weights[i] // pool), spare)
            counts[i] = counts[i] + more
            spare = spare - more
    return np.array([most] + counts)


def ragged_sizes(own_key, number_of, total, bound, slope):
    if number_of == 2:
        one = jax.random.randint(own_key, (), max(1, total - bound), min(bound, total - 1) + 1)
        return jnp.stack([one, total - one])
    tallies = jnp.asarray(length_profile(number_of, total, bound, slope), jnp.int32)
    pairs = (number_of - 1) // 2
    giver, sink = tallies[1:1 + 2 * pairs:2], tallies[2:2 + 2 * pairs:2]
    margin = jnp.minimum(giver - 1, bound - sink)
    shifted = jax.random.randint(jax.random.fold_in(own_key, 1), (pairs,), 0, 1 << 20) % (margin + 1)
    tallies = tallies.at[1:1 + 2 * pairs:2].set(giver - shifted).at[2:2 + 2 * pairs:2].set(sink + shifted)
    return tallies[jax.random.permutation(jax.random.fold_in(own_key, 2), number_of)]


def bell_draw(key, dims, scale, reach, shards=(), kind=jnp.bfloat16):
    drawn = jax.random.normal(key, dims, jnp.float32) * scale
    if len(shards) > 0:
        drawn = level_of(key, dims, shards, -0.22, 0.18) * drawn
    return jnp.clip(drawn, min=-reach, max=reach).astype(kind)


def setup_inputs(seed: int = 0) -> dict:
    streams_of = jax.random.split(jax.random.key(seed), 15)
    inputs = bell_draw(streams_of[0], (TOKENS, D), 1.0, 6.0, ((0, 32),), jnp.float32)
    doc_ids = jax.vmap(lambda own: jnp.searchsorted(jnp.cumsum(ragged_sizes(own, DOCS, TOK_DEV, MOST, 0)), jnp.arange(TOK_DEV), side="right"))(jax.random.split(streams_of[1], SEQS)).reshape((SEQS, TOK_DEV)).astype(jnp.int32)
    cotangent = bell_draw(streams_of[2], (TOKENS, D), 1.0, 6.0, ((0, 32),), jnp.float32)
    norm1_gain = jnp.clip(1.0 + 0.15 * jax.random.normal(streams_of[3], (D,), jnp.float32), 0.25, 1.75)
    norm2_gain = jnp.clip(1.0 + 0.15 * jax.random.normal(streams_of[4], (D,), jnp.float32), 0.25, 1.75)
    qnorm_gain = jnp.clip(1.0 + 0.15 * jax.random.normal(streams_of[5], (HEAD,), jnp.float32), 0.25, 1.75)
    knorm_gain = jnp.clip(1.0 + 0.15 * jax.random.normal(streams_of[6], (HEAD,), jnp.float32), 0.25, 1.75)
    q_weight = bell_draw(streams_of[7], (D, H * HEAD), D ** -0.5, 0.1875, ((1, 4),))
    k_weight = bell_draw(streams_of[8], (D, KV * HEAD), D ** -0.5, 0.1875, ((1, 4),))
    v_weight = bell_draw(streams_of[9], (D, KV * HEAD), D ** -0.5, 0.1875, ((1, 4),))
    o_weight = bell_draw(streams_of[10], (H * HEAD, D), (H * HEAD // 16) ** -0.5, 0.75, ((0, 4),))
    gate_weight = bell_draw(streams_of[11], (D, FF), D ** -0.5, 0.1875, ((1, 4),))
    up_weight = bell_draw(streams_of[12], (D, FF), D ** -0.5, 0.1875, ((1, 4),))
    down_weight = bell_draw(streams_of[13], (FF, D), FF ** -0.5, 0.09375, ((0, 4),))
    return {"inputs": inputs, "doc_ids": doc_ids, "cotangent": cotangent, "norm1_gain": norm1_gain, "norm2_gain": norm2_gain, "qnorm_gain": qnorm_gain, "knorm_gain": knorm_gain, "q_weight": q_weight, "k_weight": k_weight, "v_weight": v_weight, "o_weight": o_weight, "gate_weight": gate_weight, "up_weight": up_weight, "down_weight": down_weight}


EPS = 1e-05
THETA = 1000000.0
HIGH = lax.Precision.HIGHEST

@jax.custom_vjp
def low(v):
    return lax.optimization_barrier(v.astype(jnp.bfloat16)).astype(jnp.float32)

@jax.custom_vjp
def low_back(v):
    return v

def low_keep(v):
    return (low(v), None)

def low_pass(kept, grad):
    return (grad,)

def back_keep(v):
    return (v, None)

def back_low(kept, grad):
    return (low(grad),)
low.defvjp(low_keep, low_pass)
low_back.defvjp(back_keep, back_low)

def product(left, right):
    return jnp.dot(left, right, preferred_element_type=jnp.float32, precision=HIGH)

def normed(field, weights):
    return field * lax.rsqrt(lax.optimization_barrier(jnp.mean(field * field, -1, keepdims=True)) + EPS) * weights

def positions(doc_row):
    length_all = doc_row.shape[0]
    positions_all = jnp.arange(length_all, dtype=jnp.int32)
    previous = jnp.concatenate([doc_row[:1] - 1, doc_row[:-1]])
    doc_starts = jnp.where(doc_row != previous, positions_all, 0).astype(jnp.int32)
    return positions_all - lax.cummax(doc_starts)

def rotate(field, where_at):
    half_dim = HEAD // 2
    frequency = THETA ** (-jnp.arange(half_dim, dtype=jnp.float32) * 2.0 / HEAD)
    angles = where_at.astype(jnp.float32)[:, None] * frequency[None, :]
    cosine = jnp.cos(angles)[:, None, :]
    sine_val = jnp.sin(angles)[:, None, :]
    first_half = field[..., :half_dim]
    second_half = field[..., half_dim:]
    return jnp.concatenate([first_half * cosine - second_half * sine_val, second_half * cosine + first_half * sine_val], -1)

def layer(parameters, seq_inputs, doc_row):
    g_one, g_two, q_gain, k_gain, w_query, w_key, w_value, w_out, w_gate, w_up, w_down = parameters
    length_all = seq_inputs.shape[0]
    where_at = positions(doc_row)
    positions_all = jnp.arange(length_all, dtype=jnp.int32)
    normed_in = low(normed(seq_inputs, g_one))
    query_raw = low_back(product(normed_in, w_query)).reshape(length_all, H, HEAD)
    key_raw = low_back(product(normed_in, w_key)).reshape(length_all, KV, HEAD)
    values = low(low_back(product(normed_in, w_value))).reshape(length_all, KV, HEAD)
    queries = low(rotate(normed(query_raw, q_gain), where_at)).reshape(length_all, KV, H // KV, HEAD)
    key_vals = low(rotate(normed(key_raw, k_gain), where_at))
    scores = jnp.einsum('qkgd,skd->kgqs', queries, key_vals, precision=HIGH) * HEAD ** (-0.5)
    scores = low_back(scores)
    allowed = (doc_row[:, None] == doc_row[None, :]) & (positions_all[None, :] <= positions_all[:, None])
    scores = jnp.where(allowed, scores, -1e+30)
    row_max = lax.optimization_barrier(jnp.max(scores, -1, keepdims=True))
    exponent = jnp.exp(scores - row_max)
    probs = exponent / lax.optimization_barrier(jnp.sum(exponent, -1, keepdims=True))
    attended = jnp.einsum('kgqs,skd->qkgd', low(probs), values, precision=HIGH)
    attended = low(low_back(attended.reshape(length_all, H * HEAD)))
    mid_stream = seq_inputs + low_back(product(attended, w_out))
    normed_mid = low(normed(mid_stream, g_two))
    gate_pre = low_back(product(normed_mid, w_gate))
    up_pre = low_back(product(normed_mid, w_up))
    activated = low(jax.nn.silu(gate_pre) * up_pre)
    return mid_stream + low_back(product(activated, w_down))

def reference(inputs, doc_ids, cotangent, norm1_gain, norm2_gain, qnorm_gain, knorm_gain, q_weight, k_weight, v_weight, o_weight, gate_weight, up_weight, down_weight):
    parameters = tuple((item.astype(jnp.float32) for item in (norm1_gain, norm2_gain, qnorm_gain, knorm_gain, q_weight, k_weight, v_weight, o_weight, gate_weight, up_weight, down_weight)))
    seq_inputs = inputs.reshape(SEQS, TOK_DEV, D)

    def run_all(params_in, stream_in):
        per_sequence = jax.checkpoint(lambda inputs_pair: layer(params_in, inputs_pair[0], inputs_pair[1]))
        return lax.map(per_sequence, (stream_in, doc_ids))
    layer_out, pull_back = jax.vjp(run_all, parameters, seq_inputs)
    grads, input_grad = pull_back(cotangent.reshape(SEQS, TOK_DEV, D))
    return (layer_out.reshape(TOKENS, D), input_grad.reshape(TOKENS, D), grads[0], grads[1], grads[2], grads[3], grads[4], grads[5], grads[6], grads[7], grads[8], grads[9], grads[10])
```

```python
import jax
import jax.numpy as jnp
from jax import lax
from jax.sharding import PartitionSpec as P

HEAD = 64


EPS = 1e-05
THETA = 1000000.0


def normed(field, weights):
    return field * lax.rsqrt(jnp.mean(field * field, -1, keepdims=True) + EPS) * weights


def positions(doc_row):
    length_all = doc_row.shape[0]
    positions_all = jnp.arange(length_all, dtype=jnp.int32)
    previous = jnp.concatenate([doc_row[:1] - 1, doc_row[:-1]])
    doc_starts = jnp.where(doc_row != previous, positions_all, 0)
    return positions_all - lax.cummax(doc_starts)


def rotate(field, where_at):
    half_dim = HEAD // 2
    frequency = THETA ** (-jnp.arange(half_dim, dtype=jnp.float32) * 2.0 / HEAD)
    angles = where_at.astype(jnp.float32)[:, None] * frequency[None, :]
    cosine = jnp.cos(angles)[:, None, :]
    sine_val = jnp.sin(angles)[:, None, :]
    first_half = field[..., :half_dim]
    second_half = field[..., half_dim:]
    return jnp.concatenate(
        [
            first_half * cosine - second_half * sine_val,
            second_half * cosine + first_half * sine_val,
        ],
        -1,
    )


def gated(gate_pre, up_pre):
    return jax.nn.silu(gate_pre) * up_pre


def dot_plain(left, right):
    return jnp.dot(left, right, preferred_element_type=jnp.float32)


def dot_left_t(left, right):
    return lax.dot_general(
        left, right, (((0,), (0,)), ((), ())), preferred_element_type=jnp.float32
    )


def dot_right_t(left, right):
    return lax.dot_general(
        left, right, (((1,), (1,)), ((), ())), preferred_element_type=jnp.float32
    )


def body(
    inputs,
    doc_ids,
    cotangent,
    norm1_gain,
    norm2_gain,
    qnorm_gain,
    knorm_gain,
    q_weight,
    k_weight,
    v_weight,
    o_weight,
    gate_weight,
    up_weight,
    down_weight,
):
    doc_full = doc_ids[0]
    full_len = doc_full.shape[0]
    where_full = positions(doc_full)
    key_ids = jnp.arange(full_len, dtype=jnp.int32)
    query_cols = q_weight.shape[1]
    key_cols = k_weight.shape[1]
    query_heads = query_cols // HEAD
    kv_heads = key_cols // HEAD
    group_size = query_heads // kv_heads
    score_scale = HEAD ** (-0.5)
    block_rows = min(512, full_len)
    block_count = full_len // block_rows
    block_starts = jnp.arange(block_count, dtype=jnp.int32) * block_rows
    normed_one, norm1_back = jax.vjp(normed, inputs, norm1_gain)
    hidden = lax.all_gather(normed_one.astype(jnp.bfloat16), "mp", axis=0, tiled=True)
    joined = jnp.concatenate([q_weight, k_weight, v_weight], 1)
    hidden, cotangent_low = lax.optimization_barrier((hidden, cotangent.astype(jnp.bfloat16)))
    grad_full = lax.all_gather(cotangent_low, "mp", axis=0, tiled=True)
    projected = dot_plain(hidden, joined)
    query_raw = projected[:, :query_cols].reshape(full_len, query_heads, HEAD)
    key_raw = projected[:, query_cols : query_cols + key_cols].reshape(full_len, kv_heads, HEAD)
    values_all = (
        projected[:, query_cols + key_cols :].astype(jnp.bfloat16).reshape(full_len, kv_heads, HEAD)
    )
    query_rot, query_back = jax.vjp(
        lambda raw_in, weights: rotate(normed(raw_in, weights), where_full), query_raw, qnorm_gain
    )
    key_rot, key_back = jax.vjp(
        lambda raw_in, weights: rotate(normed(raw_in, weights), where_full), key_raw, knorm_gain
    )
    queries = query_rot.astype(jnp.bfloat16).reshape(full_len, kv_heads, group_size, HEAD)
    keys_all = key_rot.astype(jnp.bfloat16)

    def scores_of(begin_row):
        query_block = lax.dynamic_slice_in_dim(queries, begin_row, block_rows, 0)
        raw_scores = (
            jnp.einsum("qkgd,skd->kgqs", query_block, keys_all, preferred_element_type=jnp.float32)
            * score_scale
        )
        row_ids = begin_row + jnp.arange(block_rows, dtype=jnp.int32)
        doc_block = lax.dynamic_slice_in_dim(doc_full, begin_row, block_rows, 0)
        allowed = (doc_block[:, None] == doc_full[None, :]) & (key_ids[None, :] <= row_ids[:, None])
        return (jnp.where(allowed, raw_scores, -1e30), query_block)

    def forward_block(begin_row):
        scores, query_block = scores_of(begin_row)
        row_max = jnp.max(scores, -1, keepdims=True)
        exponent = jnp.exp(scores - row_max)
        row_total = jnp.sum(exponent, -1, keepdims=True)
        probs = (exponent / row_total).astype(jnp.bfloat16)
        block_out = jnp.einsum(
            "kgqs,skd->qkgd", probs, values_all, preferred_element_type=jnp.float32
        )
        return (block_out, (row_max + jnp.log(row_total))[..., 0])

    block_out, log_totals = lax.map(forward_block, block_starts)
    attended = block_out.reshape(full_len, query_cols).astype(jnp.bfloat16)
    mid_rows = inputs + lax.psum_scatter(
        dot_plain(attended, o_weight).astype(jnp.bfloat16), "mp", scatter_dimension=0, tiled=True
    ).astype(jnp.float32)
    normed_two, norm2_back = jax.vjp(normed, mid_rows, norm2_gain)
    hidden_mid = lax.all_gather(normed_two.astype(jnp.bfloat16), "mp", axis=0, tiled=True)
    gate_pre = dot_plain(hidden_mid, gate_weight)
    up_pre = dot_plain(hidden_mid, up_weight)
    activated, gated_back = jax.vjp(gated, gate_pre, up_pre)
    act_low = activated.astype(jnp.bfloat16)
    result = mid_rows + lax.psum_scatter(
        dot_plain(act_low, down_weight).astype(jnp.bfloat16), "mp", scatter_dimension=0, tiled=True
    ).astype(jnp.float32)
    grad_act = dot_right_t(grad_full, down_weight)
    down_wgrad = dot_left_t(act_low, grad_full)
    grad_gate, grad_up = gated_back(grad_act)
    grad_gate = grad_gate.astype(jnp.bfloat16)
    grad_up = grad_up.astype(jnp.bfloat16)
    gate_wgrad = dot_left_t(hidden_mid, grad_gate)
    up_wgrad = dot_left_t(hidden_mid, grad_up)
    grad_normed_mid = lax.psum_scatter(
        (dot_right_t(grad_gate, gate_weight) + dot_right_t(grad_up, up_weight)).astype(jnp.bfloat16),
        "mp",
        scatter_dimension=0,
        tiled=True,
    ).astype(jnp.float32)
    down_total, gate_total, up_total = lax.psum(
        (
            down_wgrad.astype(jnp.bfloat16),
            gate_wgrad.astype(jnp.bfloat16),
            up_wgrad.astype(jnp.bfloat16),
        ),
        "dp",
    )
    grad_mid_norm, gain2_grad = norm2_back(grad_normed_mid)
    grad_mid = cotangent + grad_mid_norm
    grad_mid_full = lax.all_gather(grad_mid.astype(jnp.bfloat16), "mp", axis=0, tiled=True)
    grad_att = (
        dot_right_t(grad_mid_full, o_weight)
        .astype(jnp.bfloat16)
        .reshape(full_len, kv_heads, group_size, HEAD)
    )
    out_wgrad = dot_left_t(attended, grad_mid_full)

    def backward_block(carried, block_in):
        grad_keys, grad_values = carried
        begin_row, log_block = block_in
        scores, query_block = scores_of(begin_row)
        probs = jnp.exp(scores - log_block[..., None])
        grad_out = lax.dynamic_slice_in_dim(grad_att, begin_row, block_rows, 0)
        grad_probs = jnp.einsum(
            "qkgd,skd->kgqs", grad_out, values_all, preferred_element_type=jnp.float32
        )
        row_delta = jnp.sum(probs * grad_probs, -1, keepdims=True)
        grad_scores = (probs * (grad_probs - row_delta)).astype(jnp.bfloat16)
        grad_query = (
            jnp.einsum("kgqs,skd->qkgd", grad_scores, keys_all, preferred_element_type=jnp.float32)
            * score_scale
        )
        grad_keys = (
            grad_keys
            + jnp.einsum(
                "kgqs,qkgd->skd", grad_scores, query_block, preferred_element_type=jnp.float32
            )
            * score_scale
        )
        grad_values = grad_values + jnp.einsum(
            "kgqs,qkgd->skd",
            probs.astype(jnp.bfloat16),
            grad_out,
            preferred_element_type=jnp.float32,
        )
        return ((grad_keys, grad_values), grad_query)

    zero_kv = jnp.zeros((full_len, kv_heads, HEAD), jnp.float32)
    (grad_keys, grad_values), grad_queries = lax.scan(
        backward_block, (zero_kv, zero_kv), (block_starts, log_totals)
    )
    grad_qraw, qgain_grad = query_back(grad_queries.reshape(full_len, query_heads, HEAD))
    grad_kraw, kgain_grad = key_back(grad_keys)
    grad_joined = jnp.concatenate(
        [
            grad_qraw.reshape(full_len, query_cols),
            grad_kraw.reshape(full_len, key_cols),
            grad_values.reshape(full_len, key_cols),
        ],
        1,
    ).astype(jnp.bfloat16)
    joined_wgrad = dot_left_t(hidden, grad_joined)
    grad_normed_in = lax.psum_scatter(
        dot_right_t(grad_joined, joined).astype(jnp.bfloat16), "mp", scatter_dimension=0, tiled=True
    ).astype(jnp.float32)
    grad_in_norm, gain1_grad = norm1_back(grad_normed_in)
    inputs_grad = grad_mid + grad_in_norm
    gains = jnp.concatenate([gain1_grad, gain2_grad, qgain_grad, kgain_grad])
    gains = jnp.sum(lax.all_gather(gains, ("dp", "mp"), axis=0), 0)
    width = gain1_grad.shape[0]
    gain_totals = (
        gains[:width],
        gains[width : 2 * width],
        gains[2 * width : 2 * width + HEAD],
        gains[2 * width + HEAD :],
    )
    joined_low, out_low, down_total = lax.optimization_barrier(
        (joined_wgrad.astype(jnp.bfloat16), out_wgrad.astype(jnp.bfloat16), down_total)
    )
    joined_wgrad, out_wgrad = lax.psum((joined_low, out_low), "dp")
    joined_wgrad = joined_wgrad.astype(jnp.float32)
    out_wgrad = out_wgrad.astype(jnp.float32)
    gate_wgrad = gate_total.astype(jnp.float32)
    up_wgrad = up_total.astype(jnp.float32)
    down_wgrad = down_total.astype(jnp.float32)
    query_wgrad = joined_wgrad[:, :query_cols]
    key_wgrad = joined_wgrad[:, query_cols : query_cols + key_cols]
    value_wgrad = joined_wgrad[:, query_cols + key_cols :]
    return (
        result,
        inputs_grad,
        gain_totals[0],
        gain_totals[1],
        gain_totals[2],
        gain_totals[3],
        query_wgrad,
        key_wgrad,
        value_wgrad,
        out_wgrad,
        gate_wgrad,
        up_wgrad,
        down_wgrad,
    )


def solution(mesh):
    in_specs = (
        P(("dp", "mp"), None),
        P("dp", None),
        P(("dp", "mp"), None),
        P(),
        P(),
        P(),
        P(),
        P(None, "mp"),
        P(None, "mp"),
        P(None, "mp"),
        P("mp", None),
        P(None, "mp"),
        P(None, "mp"),
        P("mp", None),
    )
    out_specs = (
        P(("dp", "mp"), None),
        P(("dp", "mp"), None),
        P(),
        P(),
        P(),
        P(),
        P(None, "mp"),
        P(None, "mp"),
        P(None, "mp"),
        P("mp", None),
        P(None, "mp"),
        P(None, "mp"),
        P("mp", None),
    )
    return jax.shard_map(body, mesh=mesh, in_specs=in_specs, out_specs=out_specs, check_vma=False)
```

```python
import functools

import jax
import jax.numpy as jnp
from jax import lax
from jax.sharding import PartitionSpec as P

HEAD = 64


EPS = 1e-05
THETA = 1000000.0


def normed(field, weights):
    return field * lax.rsqrt(jnp.mean(field * field, -1, keepdims=True) + EPS) * weights


def positions(doc_row):
    length_all = doc_row.shape[0]
    positions_all = jnp.arange(length_all, dtype=jnp.int32)
    previous = jnp.concatenate([doc_row[:1] - 1, doc_row[:-1]])
    doc_starts = jnp.where(doc_row != previous, positions_all, 0)
    return positions_all - lax.cummax(doc_starts)


def rotate(field, where_at):
    half_dim = HEAD // 2
    frequency = THETA ** (-jnp.arange(half_dim, dtype=jnp.float32) * 2.0 / HEAD)
    angles = where_at.astype(jnp.float32)[:, None] * frequency[None, :]
    cosine = jnp.cos(angles)[:, None, :]
    sine_val = jnp.sin(angles)[:, None, :]
    first_half = field[..., :half_dim]
    second_half = field[..., half_dim:]
    return jnp.concatenate(
        [
            first_half * cosine - second_half * sine_val,
            second_half * cosine + first_half * sine_val,
        ],
        -1,
    )


def gated(gate_pre, up_pre):
    return jax.nn.silu(gate_pre) * up_pre


def dot_plain(left, right):
    return jnp.dot(left, right, preferred_element_type=jnp.float32)


def dot_left_t(left, right):
    return lax.dot_general(
        left, right, (((0,), (0,)), ((), ())), preferred_element_type=jnp.float32
    )


def dot_right_t(left, right):
    return lax.dot_general(
        left, right, (((1,), (1,)), ((), ())), preferred_element_type=jnp.float32
    )


def gather_rows(block, shift_count):
    blocks = [block]
    for shift in range(1, shift_count):
        pairs = [(i, (i + shift) % shift_count) for i in range(shift_count)]
        blocks.append(lax.ppermute(block, "mp", pairs))
    return jnp.concatenate(blocks, 0)


def scatter_rows(block_of, shift_count):
    order = sorted(range(1, shift_count), key=lambda shift: abs(2 * shift - shift_count))
    total = 0.0
    for shift in order:
        pairs = [(i, (i - shift) % shift_count) for i in range(shift_count)]
        sent = lax.ppermute(block_of(shift).astype(jnp.bfloat16), "mp", pairs)
        total = total + sent.astype(jnp.float32)
    return total + block_of(0)


def butterfly(field, axis, size):
    step = 1
    while step < size:
        field = field + lax.ppermute(field, axis, [(i, i ^ step) for i in range(size)])
        step *= 2
    return field


def body(
    mp_size,
    dp_size,
    inputs,
    doc_ids,
    cotangent,
    norm1_gain,
    norm2_gain,
    qnorm_gain,
    knorm_gain,
    q_weight,
    k_weight,
    v_weight,
    o_weight,
    gate_weight,
    up_weight,
    down_weight,
):
    own_rows = inputs.shape[0]
    full_len = doc_ids.shape[1]
    turn = (lax.axis_index("mp") - jnp.arange(mp_size, dtype=jnp.int32)) % mp_size

    def in_turn(field):
        return field.reshape(mp_size, own_rows)[turn].reshape(full_len)

    where_full = in_turn(positions(doc_ids[0]))
    doc_full = in_turn(doc_ids[0])
    key_ids = in_turn(jnp.arange(full_len, dtype=jnp.int32))
    query_cols = q_weight.shape[1]
    key_cols = k_weight.shape[1]
    query_heads = query_cols // HEAD
    kv_heads = key_cols // HEAD
    group_size = query_heads // kv_heads
    score_scale = HEAD ** (-0.5)
    block_rows = min(512, full_len)
    block_count = full_len // block_rows
    block_starts = jnp.arange(block_count, dtype=jnp.int32) * block_rows
    normed_one, norm1_back = jax.vjp(normed, inputs, norm1_gain)
    hidden = gather_rows(normed_one.astype(jnp.bfloat16), mp_size)
    joined = jnp.concatenate([q_weight, k_weight, v_weight], 1)
    hidden, cotangent_low = lax.optimization_barrier((hidden, cotangent.astype(jnp.bfloat16)))
    grad_full = gather_rows(cotangent_low, mp_size)
    projected = dot_plain(hidden, joined)
    query_raw = projected[:, :query_cols].reshape(full_len, query_heads, HEAD)
    key_raw = projected[:, query_cols : query_cols + key_cols].reshape(full_len, kv_heads, HEAD)
    values_all = (
        projected[:, query_cols + key_cols :].astype(jnp.bfloat16).reshape(full_len, kv_heads, HEAD)
    )
    query_rot, query_back = jax.vjp(
        lambda raw_in, weights: rotate(normed(raw_in, weights), where_full), query_raw, qnorm_gain
    )
    key_rot, key_back = jax.vjp(
        lambda raw_in, weights: rotate(normed(raw_in, weights), where_full), key_raw, knorm_gain
    )
    queries = query_rot.astype(jnp.bfloat16).reshape(full_len, kv_heads, group_size, HEAD)
    keys_all = key_rot.astype(jnp.bfloat16)

    def scores_of(begin_row):
        query_block = lax.dynamic_slice_in_dim(queries, begin_row, block_rows, 0)
        raw_scores = (
            jnp.einsum("qkgd,skd->kgqs", query_block, keys_all, preferred_element_type=jnp.float32)
            * score_scale
        )
        row_ids = lax.dynamic_slice_in_dim(key_ids, begin_row, block_rows, 0)
        doc_block = lax.dynamic_slice_in_dim(doc_full, begin_row, block_rows, 0)
        allowed = (doc_block[:, None] == doc_full[None, :]) & (key_ids[None, :] <= row_ids[:, None])
        return (jnp.where(allowed, raw_scores, -1e30), query_block)

    def forward_block(begin_row):
        scores, query_block = scores_of(begin_row)
        row_max = jnp.max(scores, -1, keepdims=True)
        exponent = jnp.exp(scores - row_max)
        row_total = jnp.sum(exponent, -1, keepdims=True)
        probs = (exponent / row_total).astype(jnp.bfloat16)
        block_out = jnp.einsum(
            "kgqs,skd->qkgd", probs, values_all, preferred_element_type=jnp.float32
        )
        return (block_out, (row_max + jnp.log(row_total))[..., 0])

    block_out, log_totals = lax.map(forward_block, block_starts)
    block_out, log_totals, grad_full = lax.optimization_barrier((block_out, log_totals, grad_full))
    attended = block_out.reshape(full_len, query_cols).astype(jnp.bfloat16)

    def rows_of(field, shift):
        return field[shift * own_rows : (shift + 1) * own_rows]

    mid_rows = inputs + scatter_rows(
        lambda shift: dot_plain(rows_of(attended, shift), o_weight), mp_size
    )
    normed_two, norm2_back = jax.vjp(normed, mid_rows, norm2_gain)
    hidden_mid = gather_rows(normed_two.astype(jnp.bfloat16), mp_size)
    gate_pre = dot_plain(hidden_mid, gate_weight)
    up_pre = dot_plain(hidden_mid, up_weight)
    activated, gated_back = jax.vjp(gated, gate_pre, up_pre)
    act_low = activated.astype(jnp.bfloat16)
    grad_act = dot_right_t(grad_full, down_weight)
    down_wgrad = dot_left_t(act_low, grad_full)
    grad_gate, grad_up = gated_back(grad_act)
    grad_gate = grad_gate.astype(jnp.bfloat16)
    grad_up = grad_up.astype(jnp.bfloat16)
    gate_wgrad = dot_left_t(hidden_mid, grad_gate)
    up_wgrad = dot_left_t(hidden_mid, grad_up)
    grad_normed_mid = scatter_rows(
        lambda shift: dot_right_t(rows_of(grad_gate, shift), gate_weight)
        + dot_right_t(rows_of(grad_up, shift), up_weight),
        mp_size,
    )
    down_total, gate_total, up_total = lax.psum(
        (
            down_wgrad.astype(jnp.bfloat16),
            gate_wgrad.astype(jnp.bfloat16),
            up_wgrad.astype(jnp.bfloat16),
        ),
        "dp",
    )
    grad_mid_norm, gain2_grad = norm2_back(grad_normed_mid)
    grad_mid = cotangent + grad_mid_norm
    grad_mid_full = gather_rows(grad_mid.astype(jnp.bfloat16), mp_size)
    grad_mid_full, act_late = lax.optimization_barrier((grad_mid_full, act_low))
    result = mid_rows + scatter_rows(
        lambda shift: dot_plain(rows_of(act_late, shift), down_weight), mp_size
    )
    grad_att = (
        dot_right_t(grad_mid_full, o_weight)
        .astype(jnp.bfloat16)
        .reshape(full_len, kv_heads, group_size, HEAD)
    )
    out_wgrad = dot_left_t(attended, grad_mid_full)

    def backward_block(carried, block_in):
        grad_keys, grad_values = carried
        begin_row, log_block = block_in
        scores, query_block = scores_of(begin_row)
        probs = jnp.exp(scores - log_block[..., None])
        grad_out = lax.dynamic_slice_in_dim(grad_att, begin_row, block_rows, 0)
        grad_probs = jnp.einsum(
            "qkgd,skd->kgqs", grad_out, values_all, preferred_element_type=jnp.float32
        )
        row_delta = jnp.sum(probs * grad_probs, -1, keepdims=True)
        grad_scores = (probs * (grad_probs - row_delta)).astype(jnp.bfloat16)
        grad_query = (
            jnp.einsum("kgqs,skd->qkgd", grad_scores, keys_all, preferred_element_type=jnp.float32)
            * score_scale
        )
        grad_keys = (
            grad_keys
            + jnp.einsum(
                "kgqs,qkgd->skd", grad_scores, query_block, preferred_element_type=jnp.float32
            )
            * score_scale
        )
        grad_values = grad_values + jnp.einsum(
            "kgqs,qkgd->skd",
            probs.astype(jnp.bfloat16),
            grad_out,
            preferred_element_type=jnp.float32,
        )
        return ((grad_keys, grad_values), grad_query)

    zero_kv = jnp.zeros((full_len, kv_heads, HEAD), jnp.float32)
    (grad_keys, grad_values), grad_queries = lax.scan(
        backward_block, (zero_kv, zero_kv), (block_starts, log_totals)
    )
    grad_queries, grad_keys, grad_values, result = lax.optimization_barrier(
        (grad_queries, grad_keys, grad_values, result)
    )
    grad_qraw, qgain_grad = query_back(grad_queries.reshape(full_len, query_heads, HEAD))
    grad_kraw, kgain_grad = key_back(grad_keys)
    grad_joined = jnp.concatenate(
        [
            grad_qraw.reshape(full_len, query_cols),
            grad_kraw.reshape(full_len, key_cols),
            grad_values.reshape(full_len, key_cols),
        ],
        1,
    ).astype(jnp.bfloat16)
    joined_wgrad = dot_left_t(hidden, grad_joined)
    grad_normed_in = scatter_rows(
        lambda shift: dot_right_t(rows_of(grad_joined, shift), joined), mp_size
    )
    joined_low, out_low, down_total, gate_total, up_total = lax.optimization_barrier(
        (
            joined_wgrad.astype(jnp.bfloat16),
            out_wgrad.astype(jnp.bfloat16),
            down_total,
            gate_total,
            up_total,
        )
    )
    grad_normed_in, _, _, _ = lax.optimization_barrier(
        (grad_normed_in, joined_low, out_low, down_total)
    )
    grad_in_norm, gain1_grad = norm1_back(grad_normed_in)
    inputs_grad = grad_mid + grad_in_norm
    gains = jnp.concatenate([gain1_grad, gain2_grad, qgain_grad, kgain_grad])
    gains = butterfly(butterfly(gains, "dp", dp_size), "mp", mp_size)
    width = gain1_grad.shape[0]
    gain_totals = (
        gains[:width],
        gains[width : 2 * width],
        gains[2 * width : 2 * width + HEAD],
        gains[2 * width + HEAD :],
    )
    joined_wgrad, out_wgrad = lax.psum((joined_low, out_low), "dp")
    joined_wgrad = joined_wgrad.astype(jnp.float32)
    out_wgrad = out_wgrad.astype(jnp.float32)
    gate_wgrad = gate_total.astype(jnp.float32)
    up_wgrad = up_total.astype(jnp.float32)
    down_wgrad = down_total.astype(jnp.float32)
    query_wgrad = joined_wgrad[:, :query_cols]
    key_wgrad = joined_wgrad[:, query_cols : query_cols + key_cols]
    value_wgrad = joined_wgrad[:, query_cols + key_cols :]
    return (
        result,
        inputs_grad,
        gain_totals[0],
        gain_totals[1],
        gain_totals[2],
        gain_totals[3],
        query_wgrad,
        key_wgrad,
        value_wgrad,
        out_wgrad,
        gate_wgrad,
        up_wgrad,
        down_wgrad,
    )


def solution(mesh):
    in_specs = (
        P(("dp", "mp"), None),
        P("dp", None),
        P(("dp", "mp"), None),
        P(),
        P(),
        P(),
        P(),
        P(None, "mp"),
        P(None, "mp"),
        P(None, "mp"),
        P("mp", None),
        P(None, "mp"),
        P(None, "mp"),
        P("mp", None),
    )
    out_specs = (
        P(("dp", "mp"), None),
        P(("dp", "mp"), None),
        P(),
        P(),
        P(),
        P(),
        P(None, "mp"),
        P(None, "mp"),
        P(None, "mp"),
        P("mp", None),
        P(None, "mp"),
        P(None, "mp"),
        P("mp", None),
    )
    local = functools.partial(body, mesh.shape["mp"], mesh.shape["dp"])
    return jax.shard_map(local, mesh=mesh, in_specs=in_specs, out_specs=out_specs, check_vma=False)
```

```python
import functools

import jax
import jax.numpy as jnp
from jax import lax
from jax.sharding import PartitionSpec as P

HEAD = 64


EPS = 1e-05
THETA = 1000000.0


def normed(field, weights):
    return field * lax.rsqrt(jnp.mean(field * field, -1, keepdims=True) + EPS) * weights


def positions(doc_row):
    length_all = doc_row.shape[0]
    positions_all = jnp.arange(length_all, dtype=jnp.int32)
    previous = jnp.concatenate([doc_row[:1] - 1, doc_row[:-1]])
    doc_starts = jnp.where(doc_row != previous, positions_all, 0)
    return positions_all - lax.cummax(doc_starts)


def rotate(field, where_at):
    half_dim = HEAD // 2
    frequency = THETA ** (-jnp.arange(half_dim, dtype=jnp.float32) * 2.0 / HEAD)
    angles = where_at.astype(jnp.float32)[:, None] * frequency[None, :]
    cosine = jnp.cos(angles)[:, None, :]
    sine_val = jnp.sin(angles)[:, None, :]
    first_half = field[..., :half_dim]
    second_half = field[..., half_dim:]
    return jnp.concatenate(
        [
            first_half * cosine - second_half * sine_val,
            second_half * cosine + first_half * sine_val,
        ],
        -1,
    )


def gated(gate_pre, up_pre):
    return jax.nn.silu(gate_pre) * up_pre


def dot_plain(left, right):
    return jnp.dot(left, right, preferred_element_type=jnp.float32)


def dot_left_t(left, right):
    return lax.dot_general(
        left, right, (((0,), (0,)), ((), ())), preferred_element_type=jnp.float32
    )


def dot_right_t(left, right):
    return lax.dot_general(
        left, right, (((1,), (1,)), ((), ())), preferred_element_type=jnp.float32
    )


def gather_rows(block, shift_count):
    blocks = [block]
    for shift in range(1, shift_count):
        pairs = [(i, (i + shift) % shift_count) for i in range(shift_count)]
        blocks.append(lax.ppermute(block, "mp", pairs))
    return jnp.concatenate(blocks, 0)


def scatter_rows(block_of, shift_count):
    order = sorted(range(1, shift_count), key=lambda shift: abs(2 * shift - shift_count))
    total = 0.0
    for shift in order:
        pairs = [(i, (i - shift) % shift_count) for i in range(shift_count)]
        sent = lax.ppermute(block_of(shift).astype(jnp.bfloat16), "mp", pairs)
        total = total + sent.astype(jnp.float32)
    return total + block_of(0)


def butterfly(field, axis, size):
    step = 1
    while step < size:
        field = field + lax.ppermute(field, axis, [(i, i ^ step) for i in range(size)])
        step *= 2
    return field


def body(
    mp_size,
    dp_size,
    inputs,
    doc_ids,
    cotangent,
    norm1_gain,
    norm2_gain,
    qnorm_gain,
    knorm_gain,
    q_weight,
    k_weight,
    v_weight,
    o_weight,
    gate_weight,
    up_weight,
    down_weight,
):
    own_rows = inputs.shape[0]
    full_len = doc_ids.shape[1]
    turn = (lax.axis_index("mp") - jnp.arange(mp_size, dtype=jnp.int32)) % mp_size

    def in_turn(field):
        return field.reshape(mp_size, own_rows)[turn].reshape(full_len)

    where_full = in_turn(positions(doc_ids[0]))
    doc_full = in_turn(doc_ids[0])
    key_ids = in_turn(jnp.arange(full_len, dtype=jnp.int32))
    query_cols = q_weight.shape[1]
    key_cols = k_weight.shape[1]
    query_heads = query_cols // HEAD
    kv_heads = key_cols // HEAD
    group_size = query_heads // kv_heads
    score_scale = HEAD ** (-0.5)
    block_rows = min(512, full_len)
    block_count = full_len // block_rows
    block_starts = jnp.arange(block_count, dtype=jnp.int32) * block_rows
    normed_one, norm1_back = jax.vjp(normed, inputs, norm1_gain)
    hidden = gather_rows(normed_one.astype(jnp.bfloat16), mp_size)
    joined = jnp.concatenate([q_weight, k_weight, v_weight], 1)
    hidden, cotangent_low = lax.optimization_barrier((hidden, cotangent.astype(jnp.bfloat16)))
    grad_full = gather_rows(cotangent_low, mp_size)
    projected = dot_plain(hidden, joined)
    query_raw = projected[:, :query_cols].reshape(full_len, query_heads, HEAD)
    key_raw = projected[:, query_cols : query_cols + key_cols].reshape(full_len, kv_heads, HEAD)
    values_all = (
        projected[:, query_cols + key_cols :].astype(jnp.bfloat16).reshape(full_len, kv_heads, HEAD)
    )
    query_rot, query_back = jax.vjp(
        lambda raw_in, weights: rotate(normed(raw_in, weights), where_full), query_raw, qnorm_gain
    )
    key_rot, key_back = jax.vjp(
        lambda raw_in, weights: rotate(normed(raw_in, weights), where_full), key_raw, knorm_gain
    )
    queries = query_rot.astype(jnp.bfloat16).reshape(full_len, kv_heads, group_size, HEAD)
    keys_all = key_rot.astype(jnp.bfloat16)

    def scores_of(begin_row):
        query_block = lax.dynamic_slice_in_dim(queries, begin_row, block_rows, 0)
        raw_scores = (
            jnp.einsum("qkgd,skd->kgqs", query_block, keys_all, preferred_element_type=jnp.float32)
            * score_scale
        )
        row_ids = lax.dynamic_slice_in_dim(key_ids, begin_row, block_rows, 0)
        doc_block = lax.dynamic_slice_in_dim(doc_full, begin_row, block_rows, 0)
        allowed = (doc_block[:, None] == doc_full[None, :]) & (key_ids[None, :] <= row_ids[:, None])
        return (jnp.where(allowed, raw_scores, -1e30), query_block)

    def forward_block(begin_row):
        scores, query_block = scores_of(begin_row)
        row_max = jnp.max(scores, -1, keepdims=True)
        exponent = jnp.exp(scores - row_max)
        row_total = jnp.sum(exponent, -1, keepdims=True)
        probs = (exponent / row_total).astype(jnp.bfloat16)
        block_out = jnp.einsum(
            "kgqs,skd->qkgd", probs, values_all, preferred_element_type=jnp.float32
        )
        return (block_out, (row_max + jnp.log(row_total))[..., 0])

    block_out, log_totals = lax.map(forward_block, block_starts)
    block_out, log_totals, grad_full = lax.optimization_barrier((block_out, log_totals, grad_full))
    attended = block_out.reshape(full_len, query_cols).astype(jnp.bfloat16)

    def rows_of(field, shift):
        return field[shift * own_rows : (shift + 1) * own_rows]

    mid_rows = inputs + scatter_rows(
        lambda shift: dot_plain(rows_of(attended, shift), o_weight), mp_size
    )
    normed_two, norm2_back = jax.vjp(normed, mid_rows, norm2_gain)
    hidden_mid = gather_rows(normed_two.astype(jnp.bfloat16), mp_size)
    gate_pre = dot_plain(hidden_mid, gate_weight)
    up_pre = dot_plain(hidden_mid, up_weight)
    activated, gated_back = jax.vjp(gated, gate_pre, up_pre)
    act_low = activated.astype(jnp.bfloat16)
    grad_act = dot_right_t(grad_full, down_weight)
    down_wgrad = dot_left_t(act_low, grad_full)
    grad_gate, grad_up = gated_back(grad_act)
    grad_gate = grad_gate.astype(jnp.bfloat16)
    grad_up = grad_up.astype(jnp.bfloat16)
    gate_wgrad = dot_left_t(hidden_mid, grad_gate)
    up_wgrad = dot_left_t(hidden_mid, grad_up)
    grad_normed_mid = scatter_rows(
        lambda shift: dot_right_t(rows_of(grad_gate, shift), gate_weight)
        + dot_right_t(rows_of(grad_up, shift), up_weight),
        mp_size,
    )
    down_total, gate_total, up_total = lax.psum(
        (
            down_wgrad.astype(jnp.bfloat16),
            gate_wgrad.astype(jnp.bfloat16),
            up_wgrad.astype(jnp.bfloat16),
        ),
        "dp",
    )
    grad_mid_norm, gain2_grad = norm2_back(grad_normed_mid)
    grad_mid = cotangent + grad_mid_norm
    grad_mid_full = gather_rows(grad_mid.astype(jnp.bfloat16), mp_size)
    grad_mid_full, act_late = lax.optimization_barrier((grad_mid_full, act_low))
    result = mid_rows + scatter_rows(
        lambda shift: dot_plain(rows_of(act_late, shift), down_weight), mp_size
    )
    grad_att = (
        dot_right_t(grad_mid_full, o_weight)
        .astype(jnp.bfloat16)
        .reshape(full_len, kv_heads, group_size, HEAD)
    )
    out_wgrad = dot_left_t(attended, grad_mid_full)

    def backward_block(carried, block_in):
        grad_keys, grad_values = carried
        begin_row, log_block = block_in
        scores, query_block = scores_of(begin_row)
        probs = jnp.exp(scores - log_block[..., None])
        grad_out = lax.dynamic_slice_in_dim(grad_att, begin_row, block_rows, 0)
        grad_probs = jnp.einsum(
            "qkgd,skd->kgqs", grad_out, values_all, preferred_element_type=jnp.float32
        )
        row_delta = jnp.sum(probs * grad_probs, -1, keepdims=True)
        grad_scores = (probs * (grad_probs - row_delta)).astype(jnp.bfloat16)
        grad_query = (
            jnp.einsum("kgqs,skd->qkgd", grad_scores, keys_all, preferred_element_type=jnp.float32)
            * score_scale
        )
        grad_keys = (
            grad_keys
            + jnp.einsum(
                "kgqs,qkgd->skd", grad_scores, query_block, preferred_element_type=jnp.float32
            )
            * score_scale
        )
        grad_values = grad_values + jnp.einsum(
            "kgqs,qkgd->skd",
            probs.astype(jnp.bfloat16),
            grad_out,
            preferred_element_type=jnp.float32,
        )
        return ((grad_keys, grad_values), grad_query)

    zero_kv = jnp.zeros((full_len, kv_heads, HEAD), jnp.float32)
    (grad_keys, grad_values), grad_queries = lax.scan(
        backward_block, (zero_kv, zero_kv), (block_starts, log_totals)
    )
    grad_queries, grad_keys, grad_values, result = lax.optimization_barrier(
        (grad_queries, grad_keys, grad_values, result)
    )
    grad_qraw, qgain_grad = query_back(grad_queries.reshape(full_len, query_heads, HEAD))
    grad_kraw, kgain_grad = key_back(grad_keys)
    grad_joined = jnp.concatenate(
        [
            grad_qraw.reshape(full_len, query_cols),
            grad_kraw.reshape(full_len, key_cols),
            grad_values.reshape(full_len, key_cols),
        ],
        1,
    ).astype(jnp.bfloat16)
    joined_wgrad = dot_left_t(hidden, grad_joined)
    joined_low, out_low, down_total, gate_total, up_total = lax.optimization_barrier(
        (
            joined_wgrad.astype(jnp.bfloat16),
            out_wgrad.astype(jnp.bfloat16),
            down_total,
            gate_total,
            up_total,
        )
    )
    joined_late, _, _, _ = lax.optimization_barrier((grad_joined, joined_low, out_low, down_total))
    grad_normed_in = scatter_rows(
        lambda shift: dot_right_t(
            rows_of(joined_late if shift in (0, mp_size - 1) else grad_joined, shift), joined
        ),
        mp_size,
    )
    grad_in_norm, gain1_grad = norm1_back(grad_normed_in)
    inputs_grad = grad_mid + grad_in_norm
    gains = jnp.concatenate([gain1_grad, gain2_grad, qgain_grad, kgain_grad])
    joined_wgrad, out_wgrad = lax.psum((joined_low, out_low), "dp")
    gains = butterfly(gains, "dp", dp_size)
    gains, joined_wgrad, out_wgrad = lax.optimization_barrier((gains, joined_wgrad, out_wgrad))
    gains = butterfly(gains, "mp", mp_size)
    width = gain1_grad.shape[0]
    gain_totals = (
        gains[:width],
        gains[width : 2 * width],
        gains[2 * width : 2 * width + HEAD],
        gains[2 * width + HEAD :],
    )
    joined_wgrad = joined_wgrad.astype(jnp.float32)
    out_wgrad = out_wgrad.astype(jnp.float32)
    gate_wgrad = gate_total.astype(jnp.float32)
    up_wgrad = up_total.astype(jnp.float32)
    down_wgrad = down_total.astype(jnp.float32)
    query_wgrad = joined_wgrad[:, :query_cols]
    key_wgrad = joined_wgrad[:, query_cols : query_cols + key_cols]
    value_wgrad = joined_wgrad[:, query_cols + key_cols :]
    return (
        result,
        inputs_grad,
        gain_totals[0],
        gain_totals[1],
        gain_totals[2],
        gain_totals[3],
        query_wgrad,
        key_wgrad,
        value_wgrad,
        out_wgrad,
        gate_wgrad,
        up_wgrad,
        down_wgrad,
    )


def solution(mesh):
    in_specs = (
        P(("dp", "mp"), None),
        P("dp", None),
        P(("dp", "mp"), None),
        P(),
        P(),
        P(),
        P(),
        P(None, "mp"),
        P(None, "mp"),
        P(None, "mp"),
        P("mp", None),
        P(None, "mp"),
        P(None, "mp"),
        P("mp", None),
    )
    out_specs = (
        P(("dp", "mp"), None),
        P(("dp", "mp"), None),
        P(),
        P(),
        P(),
        P(),
        P(None, "mp"),
        P(None, "mp"),
        P(None, "mp"),
        P("mp", None),
        P(None, "mp"),
        P(None, "mp"),
        P("mp", None),
    )
    local = functools.partial(body, mesh.shape["mp"], mesh.shape["dp"])
    return jax.shard_map(local, mesh=mesh, in_specs=in_specs, out_specs=out_specs, check_vma=False)
```
